128 devices in a mesh: pre: 4 (over x), head: 8 (over y, core), cache: 4 (over z).
Axes of the slice: x: 4, y: 4, z: 4, core: 2. Of those that a mesh axis runs over, the one named last changes fastest.
Arguments:
- prompt_kv: bfloat16 [16, 8, 128, 128, 256], P('cache', 'head', 'pre'), may hold values from -12 to 12
- kept: int32 [16, 8, 4, 8], P('cache', 'head', 'pre'), may hold values from 0 to 31, as said below
- live_count: int32 [16, 8], P('cache', 'head'), may hold values from 1 to 8, as said below
- queries: bfloat16 [3, 4, 4, 8192], P(None, None, 'pre', 'head'), may hold values from -8 to 8
- out_weight: bfloat16 [8192, 8, 4, 256], P('head', None, 'cache'), may hold values from -0.25 to 0.25
- prefill_x: bfloat16 [8192, 8192], P(('pre', 'cache')), may hold values from -6 to 6
- prefill_gain: bfloat16 [8192], replicated, may hold values from 0.099609375 to 1.8984375
- kv_weight: bfloat16 [8192, 8, 256], P(None, 'head'), may hold values from -0.0625 to 0.0625
Outputs:
- attended: bfloat16 [3, 4, 4, 8192], P(None, None, 'pre', ('head', 'cache'))
- next_kv: bfloat16 [8192, 8, 256], P(('pre', 'cache'), 'head')
The draws below stay inside these ranges and needn't reach their ends.
Inputs may be any that keep to these rules, and one draw needn't show every extreme that they name: `kept`: within one request, KV head and section the 8 block numbers are distinct. The first live_count entries of each section's list are live; every draw has a head with all 8 entries live.
All inputs are finite; a program needn't handle non-finite values.
Results may differ from the reference program's by a relative error of at most 0.02.
Values may be sent and summed in bfloat16 or wider, within the bound.
No kernel may reach another device: no remote copies, remote signals or barrier semaphores. Data moves between devices by JAX's collectives and lax.ppermute only.
A program may use at most 128 MiB of HBM per device.

```python
import math
import jax
import jax.numpy as jnp
from jax import lax

D = 8192
HQ = 64
KVH = 8
HD = 128
BLK = 128
PBLK_SEC = 32
KS = 8
RU = 1
STEPS = 3
SECTIONS = 4
GROUPS = 4
REQS = 16
PF_TOK = 8192
OUT_SHARD = 256
N_HEAD = 8
N_CACHE = 4


def draw_prompt_kv(key, part):
    key = jax.random.fold_in(key, 3)
    first_key = jax.random.fold_in(key, 0)
    shape = (REQS, KVH, SECTIONS * PBLK_SEC, BLK, 2 * HD)
    base = jnp.clip(jax.random.normal(first_key, shape, jnp.float32), -4.0, 4.0)
    return base.astype(jnp.bfloat16)


def draw_queries(key, part):
    key = jax.random.fold_in(key, 7)
    first_key = jax.random.fold_in(key, 0)
    shape = (STEPS, GROUPS, SECTIONS * RU, HQ, HD)
    base = jnp.clip(2.0 * jax.random.normal(first_key, shape, jnp.float32), -8.0, 8.0)
    return base.reshape(STEPS, GROUPS, SECTIONS * RU, HQ * HD).astype(jnp.bfloat16)


def draw_kept(key, part):
    key = jax.random.fold_in(key, 11)
    shape = (REQS, KVH, SECTIONS, PBLK_SEC)
    scores = jax.random.randint(key, shape, 0, 1 << 20) * PBLK_SEC + jax.lax.broadcasted_iota(jnp.int32, shape, 3)
    ordered = jnp.argsort(scores, axis=-1)
    return ordered[..., :KS].astype(jnp.int32)


def draw_live_count(key, part):
    key = jax.random.fold_in(key, 13)
    first_key, second_key = jax.random.split(key)
    drawn = jax.random.randint(first_key, (REQS, KVH), 1, KS + 1)
    chosen_spot = jax.random.randint(second_key, (), 0, REQS * KVH)
    flat_index = jnp.arange(REQS * KVH, dtype=jnp.int32).reshape(REQS, KVH)
    return jnp.where(flat_index == chosen_spot, KS, drawn).astype(jnp.int32)


def level_of(rng, dims, pieces, smallest, high):
    def one(axis_at, blocks):
        heights = jax.random.uniform(jax.random.fold_in(jax.random.fold_in(rng, 6), axis_at), (blocks,), jnp.float32, smallest / len(pieces), high / len(pieces))
        return jnp.repeat(jnp.exp(heights), dims[axis_at] // blocks).reshape((-1,) + (1,) * (len(dims) - axis_at - 1))

    factor_of = one(*pieces[0])
    for cut in pieces[1:]:
        factor_of = factor_of * one(*cut)
    return factor_of


def noise(key, extent, scale, bound, cuts=(), kind=jnp.bfloat16):
    array = scale * jax.random.normal(key, extent, jnp.float32)
    if cuts:
        array = array * level_of(key, extent, cuts, -0.22, 0.18)
    return jnp.clip(array, -bound, bound).astype(kind)


def setup_inputs(seed: int = 0) -> dict:
    splits = jax.random.split(jax.random.key(seed), 9)
    return {
        "prompt_kv": draw_prompt_kv(jax.random.fold_in(splits[8], 71), 0),
        "kept": draw_kept(jax.random.fold_in(splits[8], 71), 0),
        "live_count": draw_live_count(jax.random.fold_in(splits[8], 71), 0),
        "queries": draw_queries(jax.random.fold_in(splits[8], 71), 0),
        "out_weight": noise(splits[4], (HQ * HD, N_HEAD, N_CACHE, OUT_SHARD), (HQ * HD // 16) ** -0.5, 0.25, ((0, 8), (2, 4))),
        "prefill_x": noise(splits[5], (PF_TOK, D), 1.0, 6.0, ((0, 16),)),
        "prefill_gain": jnp.clip(1.0 + 0.18 * jax.random.normal(splits[6], (D,), jnp.float32), 0.099609375, 1.8984375).astype(jnp.bfloat16),
        "kv_weight": noise(splits[7], (D, KVH, 2 * HD), D ** -0.5, 0.0625, ((1, 8),)),
    }


def attend_one(packed):
    query_rows, key_rows, values, live_mask = packed
    factor = 1.0 / math.sqrt(HD)
    scores = jnp.einsum('shgd,htd->shgt', query_rows.astype(jnp.float32), key_rows.astype(jnp.float32)) * factor
    scores = jnp.where(live_mask[None, :, None, :], scores, jnp.float32(-1e+30))
    maxima = lax.optimization_barrier(jnp.max(scores, axis=-1, keepdims=True))
    exp_terms = jnp.exp(scores - maxima)
    totals = lax.optimization_barrier(jnp.sum(exp_terms, axis=-1))
    probs = lax.optimization_barrier(exp_terms.astype(jnp.bfloat16)).astype(jnp.float32)
    weighted = jnp.einsum('shgt,htd->shgd', probs, values.astype(jnp.float32))
    return (weighted / totals[..., None]).astype(jnp.bfloat16)

def reference(prompt_kv, kept, live_count, queries, out_weight, prefill_x, prefill_gain, kv_weight):
    offsets = (jnp.arange(SECTIONS, dtype=jnp.int32) * PBLK_SEC)[None, None, :, None]
    block_index = (kept + offsets).astype(jnp.int32).reshape(REQS, KVH, SECTIONS * KS)
    picked = jnp.take_along_axis(prompt_kv, block_index[:, :, :, None, None], axis=2)
    tokens = SECTIONS * KS * BLK
    key_rows = picked[..., :HD].reshape(REQS, KVH, tokens, HD)
    values = picked[..., HD:].reshape(REQS, KVH, tokens, HD)
    entries = jnp.arange(KS, dtype=jnp.int32)
    live_mask = entries[None, None, :] < live_count[:, :, None]
    live_mask = jnp.broadcast_to(live_mask[:, :, None, :, None], (REQS, KVH, SECTIONS, KS, BLK)).reshape(REQS, KVH, tokens)
    query_rows = queries.reshape(STEPS, REQS, KVH, HQ // KVH, HD).transpose(1, 0, 2, 3, 4)
    attention = lax.map(attend_one, (query_rows, key_rows, values, live_mask))
    attention = attention.transpose(1, 0, 2, 3, 4).reshape(STEPS * REQS, HQ * HD)
    attended = jnp.dot(attention, out_weight.reshape(HQ * HD, D), preferred_element_type=jnp.float32)
    attended = attended.astype(jnp.bfloat16).reshape(STEPS, GROUPS, SECTIONS * RU, D)
    floats = prefill_x.astype(jnp.float32)
    inverse = lax.rsqrt(lax.optimization_barrier(jnp.mean(floats * floats, axis=-1, keepdims=True)) + 1e-05)
    normed = (floats * inverse * prefill_gain.astype(jnp.float32)).astype(jnp.bfloat16)
    next_kv = jnp.dot(normed, kv_weight.reshape(D, KVH * 2 * HD), preferred_element_type=jnp.float32)
    next_kv = next_kv.astype(jnp.bfloat16).reshape(PF_TOK, KVH, 2 * HD)
    return (attended, next_kv)
```

```python
import functools
import math

import jax
import jax.numpy as jnp
from jax import lax
from jax.experimental import pallas as pl
from jax.experimental.pallas import tpu as pltpu
from jax.sharding import PartitionSpec as P

F32 = jnp.float32
BF16 = jnp.bfloat16
VMEM = pl.BlockSpec(memory_space=pltpu.VMEM)
SMEM = pl.BlockSpec(memory_space=pltpu.SMEM)
ANY = pl.BlockSpec(memory_space=pl.ANY)

PRE, HEAD, CACHE = 4, 8, 4
STEPS = 3
SLOT = 4
GROUP = 8
HD = 128
BLK = 128
KS = 8
EPS = 1e-05


def prefill_kernel(x_ref, gain_ref, w_ref, out_ref, acc, squares):
    step = pl.program_id(0)

    @pl.when(step == 0)
    def _():
        acc[...] = jnp.zeros_like(acc)
        squares[...] = jnp.zeros_like(squares)

    x = x_ref[...]
    floats = x.astype(F32)
    sq = floats * floats
    part = squares[...]
    for k in range(x.shape[1] // 128):
        part = part + sq[:, k * 128 : (k + 1) * 128]
    squares[...] = part
    acc[...] += jnp.dot(x * gain_ref[...], w_ref[...], preferred_element_type=F32)

    @pl.when(step == pl.num_programs(0) - 1)
    def _():
        mean = jnp.sum(squares[...], axis=1, keepdims=True) * (1.0 / 8192.0)
        out_ref[...] = (acc[...] * lax.rsqrt(mean + EPS)).astype(BF16)


def prefill(x, gain, w):
    rows, width = x.shape
    cols = w.shape[1]
    depth = 1024
    return pl.pallas_call(
        prefill_kernel,
        grid=(width // depth,),
        in_specs=[
            pl.BlockSpec((rows, depth), lambda k: (0, k)),
            pl.BlockSpec((1, depth), lambda k: (0, k)),
            pl.BlockSpec((depth, cols), lambda k: (k, 0)),
        ],
        out_specs=pl.BlockSpec((rows, cols), lambda k: (0, 0)),
        out_shape=jax.ShapeDtypeStruct((rows, cols), BF16),
        scratch_shapes=[pltpu.VMEM((rows, cols), F32), pltpu.VMEM((rows, 128), F32)],
        compiler_params=pltpu.CompilerParams(vmem_limit_bytes=32 * 1024 * 1024),
        cost_estimate=pl.CostEstimate(
            flops=2 * rows * width * cols,
            bytes_accessed=2 * (rows * width + width * cols + rows * cols),
            transcendentals=0,
        ),
        name="prefill",
    )(x, gain, w)


def attend_kernel(kept, live, q0, q1, q2, q3, kv_hbm, out_ref, kv, qs, sems):
    mine = lax.axis_index("pre")
    group = lax.axis_index("cache")
    copies = []
    for k in range(PRE):
        request = mine ^ k
        row = []
        for t in range(KS):
            copy = pltpu.make_async_copy(
                kv_hbm.at[request, 0, kept[request, t]], kv.at[k, t], sems.at[k, t]
            )
            copy.start()
            row.append(copy)
        copies.append(row)
    rows = GROUP * SLOT
    lane = lax.broadcasted_iota(jnp.int32, (rows, HD), 1)
    step_of = lax.broadcasted_iota(jnp.int32, (rows, HD), 0) % SLOT
    token = lax.broadcasted_iota(jnp.int32, (rows, KS * BLK), 1)
    at_group = lax.broadcasted_iota(jnp.int32, (STEPS, CACHE, GROUP * HD), 1) == group
    for k, q_ref in enumerate((q0, q1, q2, q3)):
        request = mine ^ k
        q = jnp.sum(jnp.where(at_group, q_ref[...].astype(F32), 0.0), axis=1)
        q = jnp.concatenate([q, jnp.zeros((SLOT - STEPS, GROUP * HD), F32)], axis=0)
        for j in range(GROUP):
            qs[k, j * SLOT : (j + 1) * SLOT, :] = q[:, j * HD : (j + 1) * HD]
        for copy in copies[k]:
            copy.wait()
        keys = kv[k, :, :, :HD].reshape(KS * BLK, HD)
        values = kv[k, :, :, HD:].reshape(KS * BLK, HD)
        scores = lax.dot_general(
            qs[k].astype(BF16), keys, (((1,), (1,)), ((), ())), preferred_element_type=F32
        ) * (1.0 / math.sqrt(HD))
        alive = token < live[request] * BLK
        scores = jnp.where(alive, scores, -1e30)
        top = jnp.max(scores, axis=1, keepdims=True).astype(BF16).astype(F32)
        terms = jnp.exp(scores - top)
        total = jnp.sum(terms, axis=1, keepdims=True)
        weighted = jnp.dot(terms.astype(BF16), values, preferred_element_type=F32) / total
        high = total.astype(BF16).astype(F32)
        figures = jnp.where(lane == step_of, top, 0.0)
        figures = jnp.where(lane == step_of + SLOT, high, figures)
        figures = jnp.where(lane == step_of + 2 * SLOT, total - high, figures)
        figures = (
            pltpu.roll(figures, 1, 0) + pltpu.roll(figures, 2, 0) + pltpu.roll(figures, 3, 0)
        )
        message = jnp.where(step_of == STEPS, figures, weighted).astype(BF16)
        for c in range(CACHE):
            out_ref[request * CACHE + c] = message


def attend(kept, live, queries, kv):
    return pl.pallas_call(
        attend_kernel,
        in_specs=[SMEM, SMEM, VMEM, VMEM, VMEM, VMEM, ANY],
        out_specs=VMEM,
        out_shape=jax.ShapeDtypeStruct((PRE * CACHE, GROUP * SLOT, HD), BF16),
        scratch_shapes=[
            pltpu.VMEM((PRE, KS, BLK, 2 * HD), BF16),
            pltpu.VMEM((PRE, GROUP * SLOT, HD), F32),
            pltpu.SemaphoreType.DMA((PRE, KS)),
        ],
        compiler_params=pltpu.CompilerParams(vmem_limit_bytes=16 * 1024 * 1024),
        cost_estimate=pl.CostEstimate(
            flops=2 * PRE * 2 * 32 * 1024 * 128, bytes_accessed=1 << 21, transcendentals=1 << 17
        ),
        name="attend",
    )(kept, live, *queries, kv)


def project_kernel(parts_ref, w_ref, out_ref, sheet):
    rows = GROUP * SLOT
    lane = lax.broadcasted_iota(jnp.int32, (rows, HD), 1)
    step_of = lax.broadcasted_iota(jnp.int32, (rows, HD), 0) % SLOT
    for c in range(CACHE):
        tops, totals, values = [], [], []
        for p in range(PRE):
            part = parts_ref[p * CACHE + c].astype(F32)
            figures = jnp.where(step_of == STEPS, part, 0.0)
            figures = (
                pltpu.roll(figures, rows - 1, 0)
                + pltpu.roll(figures, rows - 2, 0)
                + pltpu.roll(figures, rows - 3, 0)
            )
            tops.append(
                jnp.sum(jnp.where(lane == step_of, figures, 0.0), axis=1, keepdims=True)
            )
            totals.append(
                jnp.sum(
                    jnp.where(
                        (lane == step_of + SLOT) | (lane == step_of + 2 * SLOT), figures, 0.0
                    ),
                    axis=1,
                    keepdims=True,
                )
            )
            values.append(part)
        top = functools.reduce(jnp.maximum, tops)
        shares = [jnp.exp(t - top) * total for t, total in zip(tops, totals)]
        scale = 1.0 / functools.reduce(jnp.add, shares)
        joined = functools.reduce(
            jnp.add, [(share * scale) * value for share, value in zip(shares, values)]
        )
        joined = jnp.where(step_of == STEPS, 0.0, joined)
        for j in range(GROUP):
            sheet[j, c * SLOT : (c + 1) * SLOT, :] = joined[j * SLOT : (j + 1) * SLOT, :]
    wide = HD * HEAD
    spread = (
        lax.broadcasted_iota(jnp.int32, (HD, wide), 1) // HEAD
        == lax.broadcasted_iota(jnp.int32, (HD, wide), 0)
    ).astype(BF16)
    repeated = jnp.dot(
        sheet[...].reshape(GROUP * CACHE * SLOT, HD).astype(BF16),
        spread,
        preferred_element_type=F32,
    ).astype(BF16)
    block = lax.broadcasted_iota(jnp.int32, (CACHE * SLOT, wide), 1) % HEAD
    total = jnp.zeros((HEAD * CACHE * SLOT, out_ref.shape[2]), F32)
    for j in range(GROUP):
        rows_j = repeated[j * CACHE * SLOT : (j + 1) * CACHE * SLOT, :]
        lhs = jnp.concatenate(
            [jnp.where(block == h, rows_j, jnp.zeros_like(rows_j)) for h in range(HEAD)], axis=0
        )
        total = total + jnp.dot(
            lhs, w_ref[j * wide : (j + 1) * wide, :], preferred_element_type=F32
        )
    out_ref[...] = total.reshape(out_ref.shape).astype(BF16)


def project(parts, weight):
    cols = weight.shape[1]
    return pl.pallas_call(
        project_kernel,
        in_specs=[VMEM, VMEM],
        out_specs=VMEM,
        out_shape=jax.ShapeDtypeStruct((HEAD, CACHE * SLOT, cols), BF16),
        scratch_shapes=[pltpu.VMEM((GROUP, CACHE * SLOT, HD), F32)],
        compiler_params=pltpu.CompilerParams(vmem_limit_bytes=24 * 1024 * 1024),
        cost_estimate=pl.CostEstimate(
            flops=2 * 128 * 8192 * 256, bytes_accessed=1 << 22, transcendentals=0
        ),
        name="project",
    )(parts, weight)


def total_kernel(terms_ref, out_ref, sheet):
    for n in range(terms_ref.shape[2] // 128):
        lanes = slice(n * 128, (n + 1) * 128)
        sheet[n] = jnp.sum(terms_ref[:, :, lanes].astype(F32), axis=0)
        for s in range(STEPS):
            out_ref[s, :, lanes] = sheet[n, pl.ds(s, CACHE, stride=SLOT), :].astype(BF16)


def total_of(terms):
    cols = terms.shape[2]
    return pl.pallas_call(
        total_kernel,
        in_specs=[VMEM],
        out_specs=VMEM,
        out_shape=jax.ShapeDtypeStruct((STEPS, CACHE, cols), BF16),
        scratch_shapes=[pltpu.VMEM((cols // 128, CACHE * SLOT, 128), F32)],
        name="total",
    )(terms)


def body(prompt_kv, kept, live_count, queries, out_weight, prefill_x, prefill_gain, kv_weight):
    queries = queries.reshape(STEPS, CACHE, GROUP * HD)
    around = [queries]
    for k in (2, 1, 3):
        around.append(lax.ppermute(queries, "pre", [(i, i ^ k) for i in range(PRE)]))
    around = [around[0], around[2], around[1], around[3]]
    parts = attend(kept.reshape(PRE, KS), live_count.reshape(PRE), around, prompt_kv)
    parts = lax.all_to_all(parts, ("pre", "cache"), split_axis=0, concat_axis=0, tiled=True)
    next_kv = prefill(prefill_x, prefill_gain.reshape(1, -1), kv_weight.reshape(8192, 256))
    terms = project(parts, out_weight.reshape(8192, 256))
    terms = lax.all_to_all(terms, "head", split_axis=0, concat_axis=0, tiled=True)
    attended = total_of(terms)
    return (attended.reshape(STEPS, CACHE, 1, 256), next_kv.reshape(512, 1, 256))


def solution(mesh):
    in_specs = (
        P("cache", "head", "pre", None, None),
        P("cache", "head", "pre", None),
        P("cache", "head"),
        P(None, None, "pre", "head"),
        P("head", None, "cache", None),
        P(("pre", "cache"), None),
        P(),
        P(None, "head", None),
    )
    out_specs = (P(None, None, "pre", ("head", "cache")), P(("pre", "cache"), "head", None))
    return jax.shard_map(body, mesh=mesh, in_specs=in_specs, out_specs=out_specs, check_vma=False)
```

```python
import functools
import math

import jax
import jax.numpy as jnp
from jax import lax
from jax.experimental import pallas as pl
from jax.experimental.pallas import tpu as pltpu
from jax.sharding import PartitionSpec as P

F32 = jnp.float32
BF16 = jnp.bfloat16
VMEM = pl.BlockSpec(memory_space=pltpu.VMEM)
SMEM = pl.BlockSpec(memory_space=pltpu.SMEM)
HBM = pl.BlockSpec(memory_space=pltpu.HBM)
ANY = pl.BlockSpec(memory_space=pl.ANY)

PRE, HEAD, CACHE = 4, 8, 4
STEPS = 3
SLOT = 4
ROWS = 16
GROUP = 8
HD = 128
BLK = 128
KS = 8
EPS = 1e-05
CHUNKS = 8
AHEAD = 4
TALL = 128
FIRST = 2
PEERS = (0, 2, 1, 3)
ORDER = (2, 1, 3)
HELD = 5


def hbm(array):
    return pltpu.with_memory_space_constraint(array, pltpu.HBM)


def vmem(array):
    return pltpu.with_memory_space_constraint(array, pltpu.VMEM)


def prefill_copies(start, x_hbm, w_hbm, x, w, x_sems, w_sems):
    depth = x.shape[2]

    def copies(k):
        lanes = pl.ds(pl.multiple_of((start + k) * depth, depth), depth)
        return [
            pltpu.make_async_copy(w_hbm.at[lanes, :], w.at[k], w_sems.at[k]),
            pltpu.make_async_copy(x_hbm.at[:, lanes], x.at[k], x_sems.at[k]),
        ]

    return copies


def prefill_steps(start, copies, gain, x, w, acc, squares):
    chunks, rows, depth = x.shape

    def step(k, carry):
        for copy in copies(k):
            copy.wait()

        @pl.when(k + AHEAD < chunks)
        def _():
            for copy in copies(k + AHEAD):
                copy.start()

        scale = gain[pl.ds(pl.multiple_of((start + k) * depth, depth), depth)].reshape(1, depth)
        for r in range(rows // TALL):
            at = slice(r * TALL, (r + 1) * TALL)
            part = squares[at, :]
            scaled = []
            for n in range(depth // 128):
                lanes = slice(n * 128, (n + 1) * 128)
                tile = x[k, at, lanes]
                floats = tile.astype(F32)
                part = part + floats * floats
                scaled.append(tile * scale[:, lanes])
            squares[at, :] = part
            acc[at, :] += jnp.dot(
                jnp.concatenate(scaled, axis=1), w[k], preferred_element_type=F32
            )
        return carry

    lax.fori_loop(0, chunks, step, 0)


def prefill_scratch(rows, width, cols, chunks):
    depth = width // CHUNKS
    return [
        pltpu.VMEM((chunks, rows, depth), BF16),
        pltpu.VMEM((chunks, depth, cols), BF16),
        pltpu.VMEM((width,), BF16),
        pltpu.SemaphoreType.DMA((chunks,)),
        pltpu.SemaphoreType.DMA((chunks,)),
        pltpu.SemaphoreType.DMA((1,)),
    ]


def begin_kernel(
    kept_hbm, live_hbm, kv_hbm, x_hbm, gain_hbm, w_hbm,
    kv, bias, acc, squares,
    kept, live, small, blocks, x, w, gain, x_sems, w_sems, gain_sem,
):
    first = pltpu.make_async_copy(kept_hbm, kept, small.at[0])
    second = pltpu.make_async_copy(live_hbm, live, small.at[1])
    third = pltpu.make_async_copy(gain_hbm, gain, gain_sem.at[0])
    first.start()
    second.start()
    third.start()
    copies = prefill_copies(0, x_hbm, w_hbm, x, w, x_sems, w_sems)
    for k in range(min(AHEAD, x.shape[0])):
        for copy in copies(k):
            copy.start()
    acc[...] = jnp.zeros_like(acc)
    squares[...] = jnp.zeros_like(squares)
    first.wait()
    arriving = []
    for i in range(PRE):
        for t in range(KS):
            copy = pltpu.make_async_copy(kv_hbm.at[i, 0, kept[i, t]], kv.at[i, t], blocks.at[i, t])
            copy.start()
            arriving.append(copy)
    second.wait()
    token = lax.broadcasted_iota(jnp.int32, (1, KS * BLK), 1)
    for i in range(PRE):
        bias[i : i + 1, :] = jnp.where(token < live[i] * BLK, 0.0, -1e30)
    third.wait()
    prefill_steps(0, copies, gain, x, w, acc, squares)
    for copy in arriving:
        copy.wait()


def begin(kept, live, kv, x, gain, w):
    rows, width = x.shape
    cols = w.shape[1]
    return pl.pallas_call(
        begin_kernel,
        in_specs=[HBM] * 6,
        out_specs=[VMEM] * 4,
        out_shape=[
            pltpu.VMEM((PRE, KS, BLK, 2 * HD), BF16),
            pltpu.VMEM((PRE, KS * BLK), F32),
            pltpu.VMEM((rows, cols), F32),
            pltpu.VMEM((rows, 128), F32),
        ],
        scratch_shapes=[
            pltpu.SMEM(kept.shape, jnp.int32),
            pltpu.SMEM(live.shape, jnp.int32),
            pltpu.SemaphoreType.DMA((2,)),
            pltpu.SemaphoreType.DMA((PRE, KS)),
            *prefill_scratch(rows, width, cols, FIRST),
        ],
        compiler_params=pltpu.CompilerParams(vmem_limit_bytes=16 * 1024 * 1024),
        cost_estimate=pl.CostEstimate(
            flops=2 * rows * width * cols * FIRST // CHUNKS,
            bytes_accessed=(2 << 20) + 2 * (rows + cols) * width * FIRST // CHUNKS,
            transcendentals=0,
        ),
        name="begin",
    )(hbm(kept), hbm(live), hbm(kv), hbm(x), hbm(gain), hbm(w))


def finish_kernel(
    x_hbm, gain_hbm, w_hbm, weight_hbm, before, before_squares, after_ref,
    out_ref, held,
    acc, squares, held_sem, x, w, gain, x_sems, w_sems, gain_sem,
):
    third = pltpu.make_async_copy(gain_hbm, gain, gain_sem.at[0])
    third.start()
    copies = prefill_copies(FIRST, x_hbm, w_hbm, x, w, x_sems, w_sems)
    for k in range(min(AHEAD, x.shape[0])):
        for copy in copies(k):
            copy.start()
    weight = pltpu.make_async_copy(weight_hbm.at[pl.ds(0, held.shape[0]), :], held, held_sem.at[0])
    weight.start()
    acc[...] = before[...]
    squares[...] = before_squares[...]
    third.wait()
    prefill_steps(FIRST, copies, gain, x, w, acc, squares)
    mean = jnp.sum(squares[...], axis=1, keepdims=True) * (1.0 / x_hbm.shape[1])
    out_ref[...] = (acc[...] * lax.rsqrt(mean + EPS)).astype(BF16)
    weight.wait()


def finish(x, gain, w, weight, before, before_squares, after):
    rows, width = x.shape
    cols = w.shape[1]
    return pl.pallas_call(
        finish_kernel,
        in_specs=[HBM] * 4 + [VMEM] * 2 + [ANY],
        out_specs=[VMEM] * 2,
        out_shape=[
            jax.ShapeDtypeStruct((rows, cols), BF16),
            pltpu.VMEM((weight.shape[0] * HELD // GROUP, weight.shape[1]), BF16),
        ],
        scratch_shapes=[
            pltpu.VMEM((rows, cols), F32),
            pltpu.VMEM((rows, 128), F32),
            pltpu.SemaphoreType.DMA((1,)),
            *prefill_scratch(rows, width, cols, CHUNKS - FIRST),
        ],
        compiler_params=pltpu.CompilerParams(vmem_limit_bytes=20 * 1024 * 1024),
        cost_estimate=pl.CostEstimate(
            flops=2 * rows * width * cols * (CHUNKS - FIRST) // CHUNKS,
            bytes_accessed=2 * (rows + cols) * width * (CHUNKS - FIRST) // CHUNKS,
            transcendentals=0,
        ),
        name="finish",
    )(hbm(x), hbm(gain), hbm(w), hbm(weight), vmem(before), vmem(before_squares), after)


def attend_kernel(q0, q1, q2, q3, kv, bias, out_ref, turned):
    mine = lax.axis_index("pre")
    group = lax.axis_index("cache")
    lane = lax.broadcasted_iota(jnp.int32, (GROUP, HD), 1)
    for k, q_ref in zip(PEERS, (q0, q1, q2, q3)):
        for s in range(STEPS):
            floats = q_ref[s].astype(F32)
            for j in range(GROUP):
                at = (k * STEPS + s) * CACHE * GROUP + j
                turned[pl.ds(at, CACHE, stride=GROUP), :] = floats[:, j * HD : (j + 1) * HD]
    scores = []
    for k in range(PRE):
        blocks = []
        for s in range(STEPS):
            at = (k * STEPS + s) * CACHE * GROUP + group * GROUP
            blocks.append(turned[pl.ds(pl.multiple_of(at, GROUP), GROUP), :])
        blocks.append(jnp.zeros((GROUP, HD), F32))
        q = jnp.concatenate(blocks, axis=0).astype(BF16)
        keys = kv[mine ^ k, :, :, :HD].reshape(KS * BLK, HD)
        scores.append(
            lax.dot_general(q, keys, (((1,), (1,)), ((), ())), preferred_element_type=F32)
        )
    tops, totals, terms = [], [], []
    for k in range(PRE):
        biased = scores[k] * (1.0 / math.sqrt(HD)) + bias[pl.ds(mine ^ k, 1), :]
        top = jnp.max(biased, axis=1, keepdims=True).astype(BF16).astype(F32)
        term = jnp.exp(biased - top)
        tops.append(top)
        totals.append(jnp.sum(term, axis=1, keepdims=True))
        terms.append(term.astype(BF16))
    for k in range(PRE):
        values = kv[mine ^ k, :, :, HD:].reshape(KS * BLK, HD)
        weighted = jnp.dot(terms[k], values, preferred_element_type=F32) / totals[k]
        high = totals[k].astype(BF16).astype(F32)
        low = totals[k] - high
        figures = jnp.zeros((GROUP, HD), F32)
        for s in range(STEPS):
            rows = slice(s * GROUP, (s + 1) * GROUP)
            figures = jnp.where(lane == s, tops[k][rows], figures)
            figures = jnp.where(lane == s + 4, high[rows], figures)
            figures = jnp.where(lane == s + 8, low[rows], figures)
        message = jnp.concatenate([weighted[: STEPS * GROUP], figures], axis=0).astype(BF16)
        for c in range(CACHE):
            out_ref[(mine ^ k) * CACHE + c] = message


def attend(queries, kv, bias):
    return pl.pallas_call(
        attend_kernel,
        in_specs=[VMEM] * 6,
        out_specs=VMEM,
        out_shape=pltpu.VMEM((PRE * CACHE, SLOT * GROUP, HD), BF16),
        scratch_shapes=[pltpu.VMEM((PRE * STEPS * CACHE * GROUP, HD), F32)],
        compiler_params=pltpu.CompilerParams(vmem_limit_bytes=4 * 1024 * 1024),
        cost_estimate=pl.CostEstimate(
            flops=2 * PRE * 2 * 32 * 1024 * 128, bytes_accessed=1 << 21, transcendentals=1 << 17
        ),
        name="attend",
    )(*queries, vmem(kv), vmem(bias))


def project_kernel(parts_ref, held, w_hbm, out_ref, sheet, w, sems):
    wide = HD * HEAD
    copies = []
    for j in range(HELD, GROUP):
        copies.append(
            pltpu.make_async_copy(
                w_hbm.at[pl.ds(j * wide, wide), :], w.at[j - HELD], sems.at[j - HELD]
            )
        )
        copies[-1].start()
    sheet[...] = jnp.zeros_like(sheet)
    for c in range(CACHE):
        parts = [parts_ref[p * CACHE + c].astype(F32) for p in range(PRE)]
        figures = [part[STEPS * GROUP :] for part in parts]
        for s in range(STEPS):
            tops = [f[:, s : s + 1] for f in figures]
            totals = [f[:, s + 4 : s + 5] + f[:, s + 8 : s + 9] for f in figures]
            top = functools.reduce(jnp.maximum, tops)
            shares = [jnp.exp(t - top) * total for t, total in zip(tops, totals)]
            scale = 1.0 / functools.reduce(jnp.add, shares)
            joined = functools.reduce(
                jnp.add,
                [
                    (share * scale) * part[s * GROUP : (s + 1) * GROUP]
                    for share, part in zip(shares, parts)
                ],
            )
            sheet[pl.ds(s * CACHE + c, GROUP, stride=ROWS), :] = joined
    spread = (
        lax.broadcasted_iota(jnp.int32, (HD, wide), 1) // HEAD
        == lax.broadcasted_iota(jnp.int32, (HD, wide), 0)
    ).astype(BF16)
    repeated = jnp.dot(
        sheet[...].astype(BF16), spread, preferred_element_type=F32
    ).astype(BF16)
    block = lax.broadcasted_iota(jnp.int32, (ROWS, wide), 1) % HEAD
    total = jnp.zeros((HEAD * ROWS, out_ref.shape[2]), F32)
    for j in range(GROUP):
        if j < HELD:
            weight = held[j * wide : (j + 1) * wide, :]
        else:
            copies[j - HELD].wait()
            weight = w[j - HELD]
        rows_j = repeated[j * ROWS : (j + 1) * ROWS, :]
        lhs = jnp.concatenate(
            [jnp.where(block == h, rows_j, jnp.zeros_like(rows_j)) for h in range(HEAD)], axis=0
        )
        total = total + jnp.dot(lhs, weight, preferred_element_type=F32)
    out_ref[...] = total.reshape(out_ref.shape).astype(BF16)


def project(parts, held, weight):
    cols = weight.shape[1]
    return pl.pallas_call(
        project_kernel,
        in_specs=[VMEM, VMEM, HBM],
        out_specs=VMEM,
        out_shape=pltpu.VMEM((HEAD, ROWS, cols), BF16),
        scratch_shapes=[
            pltpu.VMEM((GROUP * ROWS, HD), F32),
            pltpu.VMEM((GROUP - HELD, HD * HEAD, cols), BF16),
            pltpu.SemaphoreType.DMA((GROUP - HELD,)),
        ],
        compiler_params=pltpu.CompilerParams(vmem_limit_bytes=8 * 1024 * 1024),
        cost_estimate=pl.CostEstimate(
            flops=2 * 128 * 8192 * 256, bytes_accessed=1 << 22, transcendentals=0
        ),
        name="project",
    )(parts, vmem(held), hbm(weight))


def total_kernel(terms_ref, out_ref):
    total = jnp.sum(terms_ref[...].astype(F32), axis=0)
    for s in range(STEPS):
        out_ref[s] = total[s * CACHE : (s + 1) * CACHE].astype(BF16)


def total_of(terms):
    cols = terms.shape[2]
    return pl.pallas_call(
        total_kernel,
        in_specs=[VMEM],
        out_specs=VMEM,
        out_shape=jax.ShapeDtypeStruct((STEPS, CACHE, cols), BF16),
        compiler_params=pltpu.CompilerParams(vmem_limit_bytes=1024 * 1024),
        name="total",
    )(terms)


def body(prompt_kv, kept, live_count, queries, out_weight, prefill_x, prefill_gain, kv_weight):
    queries = queries.reshape(STEPS, CACHE, GROUP * HD)
    around = {0: queries}
    for k in ORDER:
        around[k] = lax.ppermute(queries, "pre", [(i, i ^ k) for i in range(PRE)])
    taken = (prefill_x, prefill_gain, kv_weight.reshape(8192, 256))
    kv, bias, *begun = begin(kept.reshape(PRE, KS), live_count.reshape(PRE), prompt_kv, *taken)
    parts = attend([around[k] for k in PEERS], kv, bias)
    sent = lax.all_to_all(parts, ("pre", "cache"), split_axis=0, concat_axis=0, tiled=True)
    weight = out_weight.reshape(8192, 256)
    next_kv, held = finish(*taken, weight, *begun, parts)
    terms = project(sent, held, weight)
    terms = lax.all_to_all(terms, "head", split_axis=0, concat_axis=0, tiled=True)
    attended = total_of(terms)
    return (attended.reshape(STEPS, CACHE, 1, 256), next_kv.reshape(512, 1, 256))


def solution(mesh):
    in_specs = (
        P("cache", "head", "pre", None, None),
        P("cache", "head", "pre", None),
        P("cache", "head"),
        P(None, None, "pre", "head"),
        P("head", None, "cache", None),
        P(("pre", "cache"), None),
        P(),
        P(None, "head", None),
    )
    out_specs = (P(None, None, "pre", ("head", "cache")), P(("pre", "cache"), "head", None))
    return jax.shard_map(body, mesh=mesh, in_specs=in_specs, out_specs=out_specs, check_vma=False)
```

```python
import functools
import math

import jax
import jax.numpy as jnp
from jax import lax
from jax.experimental import pallas as pl
from jax.experimental.pallas import tpu as pltpu
from jax.sharding import PartitionSpec as P

F32 = jnp.float32
BF16 = jnp.bfloat16
VMEM = pl.BlockSpec(memory_space=pltpu.VMEM)
SMEM = pl.BlockSpec(memory_space=pltpu.SMEM)
HBM = pl.BlockSpec(memory_space=pltpu.HBM)
ANY = pl.BlockSpec(memory_space=pl.ANY)

PRE, HEAD, CACHE = 4, 8, 4
STEPS = 3
SLOT = 4
ROWS = 16
GROUP = 8
HD = 128
BLK = 128
KS = 8
EPS = 1e-05
CHUNKS = 8
AHEAD = 3
TALL = 128
PEERS = (0, 1, 2, 3)
HELD = 6


def hbm(array):
    return pltpu.with_memory_space_constraint(array, pltpu.HBM)


def vmem(array):
    return pltpu.with_memory_space_constraint(array, pltpu.VMEM)


def prefill_copies(x_hbm, w_hbm, x, w, x_sems, w_sems):
    depth = x.shape[2]

    def copies(k):
        lanes = pl.ds(pl.multiple_of(k * depth, depth), depth)
        return [
            pltpu.make_async_copy(w_hbm.at[lanes, :], w.at[k], w_sems.at[k]),
            pltpu.make_async_copy(x_hbm.at[:, lanes], x.at[k], x_sems.at[k]),
        ]

    return copies


def prefill_steps(copies, gain, x, w, acc, squares, weight):
    chunks, rows, depth = x.shape

    def step(k, carry):
        for copy in copies(k):
            copy.wait()

        @pl.when(k + AHEAD < chunks)
        def _():
            for copy in copies(k + AHEAD):
                copy.start()

        @pl.when(k == 4)
        def _():
            weight.start()

        scale = gain[pl.ds(pl.multiple_of(k * depth, depth), depth)].reshape(1, depth)
        for r in range(rows // TALL):
            at = slice(r * TALL, (r + 1) * TALL)
            part = squares[at, :]
            scaled = []
            for n in range(depth // 128):
                lanes = slice(n * 128, (n + 1) * 128)
                tile = x[k, at, lanes]
                floats = tile.astype(F32)
                part = part + floats * floats
                scaled.append(tile * scale[:, lanes])
            squares[at, :] = part
            acc[at, :] += jnp.dot(
                jnp.concatenate(scaled, axis=1), w[k], preferred_element_type=F32
            )
        return carry

    lax.fori_loop(0, chunks, step, 0)


def load_kernel(kept_hbm, live_hbm, kv_hbm, kv, bias, kept, live, small, blocks):
    first = pltpu.make_async_copy(kept_hbm, kept, small.at[0])
    second = pltpu.make_async_copy(live_hbm, live, small.at[1])
    first.start()
    second.start()
    first.wait()
    arriving = []
    for i in range(PRE):
        for t in range(KS):
            copy = pltpu.make_async_copy(kv_hbm.at[i, 0, kept[i, t]], kv.at[i, t], blocks.at[i, t])
            copy.start()
            arriving.append(copy)
    second.wait()
    token = lax.broadcasted_iota(jnp.int32, (1, KS * BLK), 1)
    for i in range(PRE):
        bias[i : i + 1, :] = jnp.where(token < live[i] * BLK, 0.0, -1e30)
    for copy in arriving:
        copy.wait()


def load(kept, live, kv):
    return pl.pallas_call(
        load_kernel,
        in_specs=[HBM] * 3,
        out_specs=[VMEM] * 2,
        out_shape=[
            pltpu.VMEM((PRE, KS, BLK, 2 * HD), BF16),
            pltpu.VMEM((PRE, KS * BLK), F32),
        ],
        scratch_shapes=[
            pltpu.SMEM(kept.shape, jnp.int32),
            pltpu.SMEM(live.shape, jnp.int32),
            pltpu.SemaphoreType.DMA((2,)),
            pltpu.SemaphoreType.DMA((PRE, KS)),
        ],
        compiler_params=pltpu.CompilerParams(vmem_limit_bytes=1024 * 1024),
        cost_estimate=pl.CostEstimate(flops=0, bytes_accessed=2 << 20, transcendentals=0),
        name="load",
    )(hbm(kept), hbm(live), hbm(kv))


def prefill_kernel(
    x_hbm, gain_hbm, w_hbm, weight_hbm, after_ref,
    out_ref, held,
    acc, squares, x, w, gain, x_sems, w_sems, sems,
):
    third = pltpu.make_async_copy(gain_hbm, gain, sems.at[0])
    third.start()
    copies = prefill_copies(x_hbm, w_hbm, x, w, x_sems, w_sems)
    for k in range(AHEAD):
        for copy in copies(k):
            copy.start()
    weight = pltpu.make_async_copy(weight_hbm.at[pl.ds(0, held.shape[0]), :], held, sems.at[1])
    acc[...] = jnp.zeros_like(acc)
    squares[...] = jnp.zeros_like(squares)
    third.wait()
    prefill_steps(copies, gain, x, w, acc, squares, weight)
    mean = jnp.sum(squares[...], axis=1, keepdims=True) * (1.0 / x_hbm.shape[1])
    out_ref[...] = (acc[...] * lax.rsqrt(mean + EPS)).astype(BF16)
    weight.wait()


def prefill(x, gain, w, weight, after):
    rows, width = x.shape
    cols = w.shape[1]
    depth = width // CHUNKS
    return pl.pallas_call(
        prefill_kernel,
        in_specs=[HBM] * 4 + [ANY],
        out_specs=[VMEM] * 2,
        out_shape=[
            jax.ShapeDtypeStruct((rows, cols), BF16),
            pltpu.VMEM((weight.shape[0] * HELD // GROUP, weight.shape[1]), BF16),
        ],
        scratch_shapes=[
            pltpu.VMEM((rows, cols), F32),
            pltpu.VMEM((rows, 128), F32),
            pltpu.VMEM((CHUNKS, rows, depth), BF16),
            pltpu.VMEM((CHUNKS, depth, cols), BF16),
            pltpu.VMEM((width,), BF16),
            pltpu.SemaphoreType.DMA((CHUNKS,)),
            pltpu.SemaphoreType.DMA((CHUNKS,)),
            pltpu.SemaphoreType.DMA((2,)),
        ],
        compiler_params=pltpu.CompilerParams(vmem_limit_bytes=20 * 1024 * 1024),
        cost_estimate=pl.CostEstimate(
            flops=2 * rows * width * cols,
            bytes_accessed=2 * (rows + cols) * width,
            transcendentals=0,
        ),
        name="prefill",
    )(hbm(x), hbm(gain), hbm(w), hbm(weight), after)


def attend_kernel(q0, q1, q2, q3, kv, bias, out_ref, turned):
    mine = lax.axis_index("pre")
    group = lax.axis_index("cache")
    lane = lax.broadcasted_iota(jnp.int32, (GROUP, HD), 1)
    for k, q_ref in zip(PEERS, (q0, q1, q2, q3)):
        for s in range(STEPS):
            floats = q_ref[s].astype(F32)
            for j in range(GROUP):
                at = (k * STEPS + s) * CACHE * GROUP + j
                turned[pl.ds(at, CACHE, stride=GROUP), :] = floats[:, j * HD : (j + 1) * HD]
    scores = []
    for k in range(PRE):
        blocks = []
        for s in range(STEPS):
            at = (k * STEPS + s) * CACHE * GROUP + group * GROUP
            blocks.append(turned[pl.ds(pl.multiple_of(at, GROUP), GROUP), :])
        blocks.append(jnp.zeros((GROUP, HD), F32))
        q = jnp.concatenate(blocks, axis=0).astype(BF16)
        keys = kv[mine ^ k, :, :, :HD].reshape(KS * BLK, HD)
        scores.append(
            lax.dot_general(q, keys, (((1,), (1,)), ((), ())), preferred_element_type=F32)
        )
    tops, totals, terms = [], [], []
    for k in range(PRE):
        biased = scores[k] * (1.0 / math.sqrt(HD)) + bias[pl.ds(mine ^ k, 1), :]
        top = jnp.max(biased, axis=1, keepdims=True).astype(BF16).astype(F32)
        term = jnp.exp(biased - top)
        tops.append(top)
        totals.append(jnp.sum(term, axis=1, keepdims=True))
        terms.append(term.astype(BF16))
    for k in range(PRE):
        values = kv[mine ^ k, :, :, HD:].reshape(KS * BLK, HD)
        weighted = jnp.dot(terms[k], values, preferred_element_type=F32) / totals[k]
        high = totals[k].astype(BF16).astype(F32)
        low = totals[k] - high
        figures = jnp.zeros((GROUP, HD), F32)
        for s in range(STEPS):
            rows = slice(s * GROUP, (s + 1) * GROUP)
            figures = jnp.where(lane == s, tops[k][rows], figures)
            figures = jnp.where(lane == s + 4, high[rows], figures)
            figures = jnp.where(lane == s + 8, low[rows], figures)
        message = jnp.concatenate([weighted[: STEPS * GROUP], figures], axis=0).astype(BF16)
        for c in range(CACHE):
            out_ref[(mine ^ k) * CACHE + c] = message


def attend(queries, kv, bias):
    return pl.pallas_call(
        attend_kernel,
        in_specs=[VMEM] * 6,
        out_specs=VMEM,
        out_shape=pltpu.VMEM((PRE * CACHE, SLOT * GROUP, HD), BF16),
        scratch_shapes=[pltpu.VMEM((PRE * STEPS * CACHE * GROUP, HD), F32)],
        compiler_params=pltpu.CompilerParams(vmem_limit_bytes=4 * 1024 * 1024),
        cost_estimate=pl.CostEstimate(
            flops=2 * PRE * 2 * 32 * 1024 * 128, bytes_accessed=1 << 21, transcendentals=1 << 17
        ),
        name="attend",
    )(*queries, vmem(kv), vmem(bias))


def project_kernel(parts_ref, held, w_hbm, out_ref, sheet, w, sems):
    wide = HD * HEAD
    copies = []
    for j in range(HELD, GROUP):
        copies.append(
            pltpu.make_async_copy(
                w_hbm.at[pl.ds(j * wide, wide), :], w.at[j - HELD], sems.at[j - HELD]
            )
        )
        copies[-1].start()
    sheet[...] = jnp.zeros_like(sheet)
    for c in range(CACHE):
        parts = [parts_ref[p * CACHE + c].astype(F32) for p in range(PRE)]
        figures = [part[STEPS * GROUP :] for part in parts]
        for s in range(STEPS):
            tops = [f[:, s : s + 1] for f in figures]
            totals = [f[:, s + 4 : s + 5] + f[:, s + 8 : s + 9] for f in figures]
            top = functools.reduce(jnp.maximum, tops)
            shares = [jnp.exp(t - top) * total for t, total in zip(tops, totals)]
            scale = 1.0 / functools.reduce(jnp.add, shares)
            joined = functools.reduce(
                jnp.add,
                [
                    (share * scale) * part[s * GROUP : (s + 1) * GROUP]
                    for share, part in zip(shares, parts)
                ],
            )
            sheet[pl.ds(s * CACHE + c, GROUP, stride=ROWS), :] = joined
    spread = (
        lax.broadcasted_iota(jnp.int32, (HD, wide), 1) // HEAD
        == lax.broadcasted_iota(jnp.int32, (HD, wide), 0)
    ).astype(BF16)
    repeated = jnp.dot(
        sheet[...].astype(BF16), spread, preferred_element_type=F32
    ).astype(BF16)
    block = lax.broadcasted_iota(jnp.int32, (ROWS, wide), 1) % HEAD
    total = jnp.zeros((HEAD * ROWS, out_ref.shape[2]), F32)
    for j in range(GROUP):
        if j < HELD:
            weight = held[j * wide : (j + 1) * wide, :]
        else:
            copies[j - HELD].wait()
            weight = w[j - HELD]
        rows_j = repeated[j * ROWS : (j + 1) * ROWS, :]
        lhs = jnp.concatenate(
            [jnp.where(block == h, rows_j, jnp.zeros_like(rows_j)) for h in range(HEAD)], axis=0
        )
        total = total + jnp.dot(lhs, weight, preferred_element_type=F32)
    out_ref[...] = total.reshape(out_ref.shape).astype(BF16)


def project(parts, held, weight):
    cols = weight.shape[1]
    return pl.pallas_call(
        project_kernel,
        in_specs=[VMEM, VMEM, HBM],
        out_specs=VMEM,
        out_shape=pltpu.VMEM((HEAD, ROWS, cols), BF16),
        scratch_shapes=[
            pltpu.VMEM((GROUP * ROWS, HD), F32),
            pltpu.VMEM((GROUP - HELD, HD * HEAD, cols), BF16),
            pltpu.SemaphoreType.DMA((GROUP - HELD,)),
        ],
        compiler_params=pltpu.CompilerParams(vmem_limit_bytes=8 * 1024 * 1024),
        cost_estimate=pl.CostEstimate(
            flops=2 * 128 * 8192 * 256, bytes_accessed=1 << 22, transcendentals=0
        ),
        name="project",
    )(parts, vmem(held), hbm(weight))


def total_kernel(terms_ref, out_ref):
    total = jnp.sum(terms_ref[...].astype(F32), axis=0)
    for s in range(STEPS):
        out_ref[s] = total[s * CACHE : (s + 1) * CACHE].astype(BF16)


def total_of(terms):
    cols = terms.shape[2]
    return pl.pallas_call(
        total_kernel,
        in_specs=[VMEM],
        out_specs=VMEM,
        out_shape=jax.ShapeDtypeStruct((STEPS, CACHE, cols), BF16),
        compiler_params=pltpu.CompilerParams(vmem_limit_bytes=1024 * 1024),
        name="total",
    )(terms)


def body(prompt_kv, kept, live_count, queries, out_weight, prefill_x, prefill_gain, kv_weight):
    queries = queries.reshape(STEPS, CACHE, GROUP * HD)
    around = {0: queries}
    for k in PEERS[1:]:
        around[k] = lax.ppermute(queries, "pre", [(i, i ^ k) for i in range(PRE)])
    kv, bias = load(kept.reshape(PRE, KS), live_count.reshape(PRE), prompt_kv)
    parts = attend([around[k] for k in PEERS], kv, bias)
    sent = lax.all_to_all(parts, ("pre", "cache"), split_axis=0, concat_axis=0, tiled=True)
    weight = out_weight.reshape(8192, 256)
    next_kv, held = prefill(
        prefill_x, prefill_gain, kv_weight.reshape(8192, 256), weight, parts
    )
    terms = project(sent, held, weight)
    terms = lax.all_to_all(terms, "head", split_axis=0, concat_axis=0, tiled=True)
    attended = total_of(terms)
    return (attended.reshape(STEPS, CACHE, 1, 256), next_kv.reshape(512, 1, 256))


def solution(mesh):
    in_specs = (
        P("cache", "head", "pre", None, None),
        P("cache", "head", "pre", None),
        P("cache", "head"),
        P(None, None, "pre", "head"),
        P("head", None, "cache", None),
        P(("pre", "cache"), None),
        P(),
        P(None, "head", None),
    )
    out_specs = (P(None, None, "pre", ("head", "cache")), P(("pre", "cache"), "head", None))
    return jax.shard_map(body, mesh=mesh, in_specs=in_specs, out_specs=out_specs, check_vma=False)
```

```python
import functools
import math

import jax
import jax.numpy as jnp
from jax import lax
from jax.experimental import pallas as pl
from jax.experimental.pallas import tpu as pltpu
from jax.sharding import PartitionSpec as P

F32 = jnp.float32
BF16 = jnp.bfloat16
VMEM = pl.BlockSpec(memory_space=pltpu.VMEM)
SMEM = pl.BlockSpec(memory_space=pltpu.SMEM)
HBM = pl.BlockSpec(memory_space=pltpu.HBM)
ANY = pl.BlockSpec(memory_space=pl.ANY)

PRE, HEAD, CACHE = 4, 8, 4
STEPS = 3
SLOT = 4
ROWS = 16
GROUP = 8
HD = 128
BLK = 128
KS = 8
EPS = 1e-05
CHUNKS = 8
AHEAD = 4
TALL = 128
FIRST = 2
TURNS = (3, 2, 1)
PEERS = (0, 2, 1, 3)
ORDER = (2, 1, 3)
HELD = 5


def hbm(array):
    return pltpu.with_memory_space_constraint(array, pltpu.HBM)


def vmem(array):
    return pltpu.with_memory_space_constraint(array, pltpu.VMEM)


def prefill_copies(start, x_hbm, w_hbm, x, w, x_sems, w_sems):
    depth = x.shape[2]

    def copies(k):
        lanes = pl.ds(pl.multiple_of((start + k) * depth, depth), depth)
        return [
            pltpu.make_async_copy(w_hbm.at[lanes, :], w.at[k], w_sems.at[k]),
            pltpu.make_async_copy(x_hbm.at[:, lanes], x.at[k], x_sems.at[k]),
        ]

    return copies


def prefill_steps(start, copies, gain, x, w, acc, squares):
    chunks, rows, depth = x.shape

    def step(k, carry):
        for copy in copies(k):
            copy.wait()

        @pl.when(k + AHEAD < chunks)
        def _():
            for copy in copies(k + AHEAD):
                copy.start()

        scale = gain[pl.ds(pl.multiple_of((start + k) * depth, depth), depth)].reshape(1, depth)
        for r in range(rows // TALL):
            at = slice(r * TALL, (r + 1) * TALL)
            part = squares[at, :]
            scaled = []
            for n in range(depth // 128):
                lanes = slice(n * 128, (n + 1) * 128)
                tile = x[k, at, lanes]
                floats = tile.astype(F32)
                part = part + floats * floats
                scaled.append(tile * scale[:, lanes])
            squares[at, :] = part
            acc[at, :] += jnp.dot(
                jnp.concatenate(scaled, axis=1), w[k], preferred_element_type=F32
            )
        return carry

    lax.fori_loop(0, chunks, step, 0)


def prefill_scratch(rows, width, cols, chunks):
    depth = width // CHUNKS
    return [
        pltpu.VMEM((chunks, rows, depth), BF16),
        pltpu.VMEM((chunks, depth, cols), BF16),
        pltpu.VMEM((width,), BF16),
        pltpu.SemaphoreType.DMA((chunks,)),
        pltpu.SemaphoreType.DMA((chunks,)),
        pltpu.SemaphoreType.DMA((1,)),
    ]


def begin_kernel(
    kept_hbm, live_hbm, kv_hbm, x_hbm, gain_hbm, w_hbm,
    kv, bias, acc, squares,
    kept, live, small, blocks, x, w, gain, x_sems, w_sems, gain_sem,
):
    first = pltpu.make_async_copy(kept_hbm, kept, small.at[0])
    second = pltpu.make_async_copy(live_hbm, live, small.at[1])
    third = pltpu.make_async_copy(gain_hbm, gain, gain_sem.at[0])
    first.start()
    second.start()
    third.start()
    copies = prefill_copies(0, x_hbm, w_hbm, x, w, x_sems, w_sems)
    for k in range(min(AHEAD, x.shape[0])):
        for copy in copies(k):
            copy.start()
    acc[...] = jnp.zeros_like(acc)
    squares[...] = jnp.zeros_like(squares)
    first.wait()
    arriving = []
    for i in range(PRE):
        for t in range(KS):
            copy = pltpu.make_async_copy(kv_hbm.at[i, 0, kept[i, t]], kv.at[i, t], blocks.at[i, t])
            copy.start()
            arriving.append(copy)
    second.wait()
    token = lax.broadcasted_iota(jnp.int32, (1, KS * BLK), 1)
    for i in range(PRE):
        bias[i : i + 1, :] = jnp.where(token < live[i] * BLK, 0.0, -1e30)
    third.wait()
    prefill_steps(0, copies, gain, x, w, acc, squares)
    for copy in arriving:
        copy.wait()


def begin(kept, live, kv, x, gain, w):
    rows, width = x.shape
    cols = w.shape[1]
    return pl.pallas_call(
        begin_kernel,
        in_specs=[HBM] * 6,
        out_specs=[VMEM] * 4,
        out_shape=[
            pltpu.VMEM((PRE, KS, BLK, 2 * HD), BF16),
            pltpu.VMEM((PRE, KS * BLK), F32),
            pltpu.VMEM((rows, cols), F32),
            pltpu.VMEM((rows, 128), F32),
        ],
        scratch_shapes=[
            pltpu.SMEM(kept.shape, jnp.int32),
            pltpu.SMEM(live.shape, jnp.int32),
            pltpu.SemaphoreType.DMA((2,)),
            pltpu.SemaphoreType.DMA((PRE, KS)),
            *prefill_scratch(rows, width, cols, FIRST),
        ],
        compiler_params=pltpu.CompilerParams(vmem_limit_bytes=16 * 1024 * 1024),
        cost_estimate=pl.CostEstimate(
            flops=2 * rows * width * cols * FIRST // CHUNKS,
            bytes_accessed=(2 << 20) + 2 * (rows + cols) * width * FIRST // CHUNKS,
            transcendentals=0,
        ),
        name="begin",
    )(hbm(kept), hbm(live), hbm(kv), hbm(x), hbm(gain), hbm(w))


def finish_kernel(
    x_hbm, gain_hbm, w_hbm, weight_hbm, before, before_squares, after_ref,
    out_ref, held,
    acc, squares, held_sem, x, w, gain, x_sems, w_sems, gain_sem,
):
    third = pltpu.make_async_copy(gain_hbm, gain, gain_sem.at[0])
    third.start()
    copies = prefill_copies(FIRST, x_hbm, w_hbm, x, w, x_sems, w_sems)
    for k in range(min(AHEAD, x.shape[0])):
        for copy in copies(k):
            copy.start()
    weight = pltpu.make_async_copy(weight_hbm.at[pl.ds(0, held.shape[0]), :], held, held_sem.at[0])
    weight.start()
    acc[...] = before[...]
    squares[...] = before_squares[...]
    third.wait()
    prefill_steps(FIRST, copies, gain, x, w, acc, squares)
    mean = jnp.sum(squares[...], axis=1, keepdims=True) * (1.0 / x_hbm.shape[1])
    out_ref[...] = (acc[...] * lax.rsqrt(mean + EPS)).astype(BF16)
    weight.wait()


def finish(x, gain, w, weight, before, before_squares, after):
    rows, width = x.shape
    cols = w.shape[1]
    return pl.pallas_call(
        finish_kernel,
        in_specs=[HBM] * 4 + [VMEM] * 2 + [ANY],
        out_specs=[VMEM] * 2,
        out_shape=[
            jax.ShapeDtypeStruct((rows, cols), BF16),
            pltpu.VMEM((weight.shape[0] * HELD // GROUP, weight.shape[1]), BF16),
        ],
        scratch_shapes=[
            pltpu.VMEM((rows, cols), F32),
            pltpu.VMEM((rows, 128), F32),
            pltpu.SemaphoreType.DMA((1,)),
            *prefill_scratch(rows, width, cols, CHUNKS - FIRST),
        ],
        compiler_params=pltpu.CompilerParams(vmem_limit_bytes=20 * 1024 * 1024),
        cost_estimate=pl.CostEstimate(
            flops=2 * rows * width * cols * (CHUNKS - FIRST) // CHUNKS,
            bytes_accessed=2 * (rows + cols) * width * (CHUNKS - FIRST) // CHUNKS,
            transcendentals=0,
        ),
        name="finish",
    )(hbm(x), hbm(gain), hbm(w), hbm(weight), vmem(before), vmem(before_squares), after)


def attend_kernel(q0, q1, q2, q3, kv, bias, out_ref, turned):
    mine = lax.axis_index("pre")
    group = lax.axis_index("cache")
    lane = lax.broadcasted_iota(jnp.int32, (GROUP, HD), 1)
    for k, q_ref in zip(PEERS, (q0, q1, q2, q3)):
        for s in range(STEPS):
            floats = q_ref[s].astype(F32)
            for j in range(GROUP):
                at = (k * STEPS + s) * CACHE * GROUP + j
                turned[pl.ds(at, CACHE, stride=GROUP), :] = floats[:, j * HD : (j + 1) * HD]
    scores = []
    for k in range(PRE):
        blocks = []
        for s in range(STEPS):
            at = (k * STEPS + s) * CACHE * GROUP + group * GROUP
            blocks.append(turned[pl.ds(pl.multiple_of(at, GROUP), GROUP), :])
        blocks.append(jnp.zeros((GROUP, HD), F32))
        q = jnp.concatenate(blocks, axis=0).astype(BF16)
        keys = kv[mine ^ k, :, :, :HD].reshape(KS * BLK, HD)
        scores.append(
            lax.dot_general(q, keys, (((1,), (1,)), ((), ())), preferred_element_type=F32)
        )
    tops, totals, terms = [], [], []
    for k in range(PRE):
        biased = scores[k] * (1.0 / math.sqrt(HD)) + bias[pl.ds(mine ^ k, 1), :]
        top = jnp.max(biased, axis=1, keepdims=True).astype(BF16).astype(F32)
        term = jnp.exp(biased - top)
        tops.append(top)
        totals.append(jnp.sum(term, axis=1, keepdims=True))
        terms.append(term.astype(BF16))
    for k in range(PRE):
        values = kv[mine ^ k, :, :, HD:].reshape(KS * BLK, HD)
        weighted = jnp.dot(terms[k], values, preferred_element_type=F32) / totals[k]
        high = totals[k].astype(BF16).astype(F32)
        low = totals[k] - high
        figures = jnp.zeros((GROUP, HD), F32)
        for s in range(STEPS):
            rows = slice(s * GROUP, (s + 1) * GROUP)
            figures = jnp.where(lane == s, tops[k][rows], figures)
            figures = jnp.where(lane == s + 4, high[rows], figures)
            figures = jnp.where(lane == s + 8, low[rows], figures)
        message = jnp.concatenate([weighted[: STEPS * GROUP], figures], axis=0).astype(BF16)
        for c in range(CACHE):
            out_ref[(mine ^ k) * CACHE + c] = message


def attend(queries, kv, bias):
    return pl.pallas_call(
        attend_kernel,
        in_specs=[VMEM] * 6,
        out_specs=VMEM,
        out_shape=pltpu.VMEM((PRE * CACHE, SLOT * GROUP, HD), BF16),
        scratch_shapes=[pltpu.VMEM((PRE * STEPS * CACHE * GROUP, HD), F32)],
        compiler_params=pltpu.CompilerParams(vmem_limit_bytes=4 * 1024 * 1024),
        cost_estimate=pl.CostEstimate(
            flops=2 * PRE * 2 * 32 * 1024 * 128, bytes_accessed=1 << 21, transcendentals=1 << 17
        ),
        name="attend",
    )(*queries, vmem(kv), vmem(bias))


def project_kernel(parts_ref, held, w_hbm, keep_ref, give_ref, sheet, w, result, sems):
    wide = HD * HEAD
    copies = []
    for j in range(HELD, GROUP):
        copies.append(
            pltpu.make_async_copy(
                w_hbm.at[pl.ds(j * wide, wide), :], w.at[j - HELD], sems.at[j - HELD]
            )
        )
        copies[-1].start()
    sheet[...] = jnp.zeros_like(sheet)
    for c in range(CACHE):
        parts = [parts_ref[p * CACHE + c].astype(F32) for p in range(PRE)]
        figures = [part[STEPS * GROUP :] for part in parts]
        for s in range(STEPS):
            tops = [f[:, s : s + 1] for f in figures]
            totals = [f[:, s + 4 : s + 5] + f[:, s + 8 : s + 9] for f in figures]
            top = functools.reduce(jnp.maximum, tops)
            shares = [jnp.exp(t - top) * total for t, total in zip(tops, totals)]
            scale = 1.0 / functools.reduce(jnp.add, shares)
            joined = functools.reduce(
                jnp.add,
                [
                    (share * scale) * part[s * GROUP : (s + 1) * GROUP]
                    for share, part in zip(shares, parts)
                ],
            )
            sheet[pl.ds(s * CACHE + c, GROUP, stride=ROWS), :] = joined
    spread = (
        lax.broadcasted_iota(jnp.int32, (HD, wide), 1) // HEAD
        == lax.broadcasted_iota(jnp.int32, (HD, wide), 0)
    ).astype(BF16)
    repeated = jnp.dot(
        sheet[...].astype(BF16), spread, preferred_element_type=F32
    ).astype(BF16)
    block = lax.broadcasted_iota(jnp.int32, (ROWS, wide), 1) % HEAD
    total = jnp.zeros((HEAD * ROWS, keep_ref.shape[2]), F32)
    for j in range(GROUP):
        if j < HELD:
            weight = held[j * wide : (j + 1) * wide, :]
        else:
            copies[j - HELD].wait()
            weight = w[j - HELD]
        rows_j = repeated[j * ROWS : (j + 1) * ROWS, :]
        lhs = jnp.concatenate(
            [jnp.where(block == h, rows_j, jnp.zeros_like(rows_j)) for h in range(HEAD)], axis=0
        )
        total = total + jnp.dot(lhs, weight, preferred_element_type=F32)
    result[...] = total
    chip, core = lax.axis_index("head") // 2, lax.axis_index("head") % 2
    for t in range(HEAD // 2):
        mine = ((chip ^ t) * 2 + core) * ROWS
        other = ((chip ^ t) * 2 + 1 - core) * ROWS
        keep_ref[t] = result[pl.ds(pl.multiple_of(mine, ROWS), ROWS), :]
        give_ref[t] = result[pl.ds(pl.multiple_of(other, ROWS), ROWS), :].astype(BF16)


def project(parts, held, weight):
    cols = weight.shape[1]
    return pl.pallas_call(
        project_kernel,
        in_specs=[VMEM, VMEM, HBM],
        out_specs=[VMEM, VMEM],
        out_shape=[
            pltpu.VMEM((HEAD // 2, ROWS, cols), F32),
            pltpu.VMEM((HEAD // 2, ROWS, cols), BF16),
        ],
        scratch_shapes=[
            pltpu.VMEM((GROUP * ROWS, HD), F32),
            pltpu.VMEM((GROUP - HELD, HD * HEAD, cols), BF16),
            pltpu.VMEM((HEAD * ROWS, cols), F32),
            pltpu.SemaphoreType.DMA((GROUP - HELD,)),
        ],
        compiler_params=pltpu.CompilerParams(vmem_limit_bytes=8 * 1024 * 1024),
        cost_estimate=pl.CostEstimate(
            flops=2 * 128 * 8192 * 256, bytes_accessed=1 << 22, transcendentals=0
        ),
        name="project",
    )(parts, vmem(held), hbm(weight))


def total_kernel(a_ref, b_ref, c_ref, d_ref, out_ref):
    total = sum(ref[...].astype(F32) for ref in (b_ref, c_ref, d_ref)) + a_ref[...].astype(F32)
    for s in range(STEPS):
        out_ref[s] = total[s * CACHE : (s + 1) * CACHE].astype(BF16)


def total_of(terms):
    cols = terms[0].shape[1]
    return pl.pallas_call(
        total_kernel,
        in_specs=[VMEM] * 4,
        out_specs=VMEM,
        out_shape=jax.ShapeDtypeStruct((STEPS, CACHE, cols), BF16),
        compiler_params=pltpu.CompilerParams(vmem_limit_bytes=1024 * 1024),
        name="total",
    )(*terms)


def body(prompt_kv, kept, live_count, queries, out_weight, prefill_x, prefill_gain, kv_weight):
    queries = queries.reshape(STEPS, CACHE, GROUP * HD)
    around = {0: queries}
    for k in ORDER:
        around[k] = lax.ppermute(queries, "pre", [(i, i ^ k) for i in range(PRE)])
    taken = (prefill_x, prefill_gain, kv_weight.reshape(8192, 256))
    kv, bias, *begun = begin(kept.reshape(PRE, KS), live_count.reshape(PRE), prompt_kv, *taken)
    parts = attend([around[k] for k in PEERS], kv, bias)
    sent = lax.all_to_all(parts, ("pre", "cache"), split_axis=0, concat_axis=0, tiled=True)
    weight = out_weight.reshape(8192, 256)
    next_kv, held = finish(*taken, weight, *begun, parts)
    keep, give = project(sent, held, weight)
    got = lax.ppermute(give, "head", [(i, i ^ 1) for i in range(HEAD)])
    pairs = (keep + got.astype(F32)).astype(BF16)
    terms = [pairs[0]]
    for t in TURNS:
        terms.append(lax.ppermute(pairs[t], "head", [(i, i ^ (2 * t)) for i in range(HEAD)]))
    attended = total_of(terms)
    return (attended.reshape(STEPS, CACHE, 1, 256), next_kv.reshape(512, 1, 256))


def solution(mesh):
    in_specs = (
        P("cache", "head", "pre", None, None),
        P("cache", "head", "pre", None),
        P("cache", "head"),
        P(None, None, "pre", "head"),
        P("head", None, "cache", None),
        P(("pre", "cache"), None),
        P(),
        P(None, "head", None),
    )
    out_specs = (P(None, None, "pre", ("head", "cache")), P(("pre", "cache"), "head", None))
    return jax.shard_map(body, mesh=mesh, in_specs=in_specs, out_specs=out_specs, check_vma=False)
```

```python
import functools
import math

import jax
import jax.numpy as jnp
from jax import lax
from jax.experimental import pallas as pl
from jax.experimental.pallas import tpu as pltpu
from jax.sharding import PartitionSpec as P

F32 = jnp.float32
BF16 = jnp.bfloat16
VMEM = pl.BlockSpec(memory_space=pltpu.VMEM)
SMEM = pl.BlockSpec(memory_space=pltpu.SMEM)
HBM = pl.BlockSpec(memory_space=pltpu.HBM)
ANY = pl.BlockSpec(memory_space=pl.ANY)

PRE, HEAD, CACHE = 4, 8, 4
STEPS = 3
SLOT = 4
ROWS = 16
GROUP = 8
HD = 128
BLK = 128
KS = 8
EPS = 1e-05
CHUNKS = 8
AHEAD = 4
TALL = 128
FIRST = 2
TURNS = ((0, 0), (2, 3), (3, 2), (1, 1))
PEERS = (0, 2, 1, 3)
ORDER = (2, 1, 3)
HELD = 5


def hbm(array):
    return pltpu.with_memory_space_constraint(array, pltpu.HBM)


def vmem(array):
    return pltpu.with_memory_space_constraint(array, pltpu.VMEM)


def prefill_copies(start, x_hbm, w_hbm, x, w, x_sems, w_sems):
    depth = x.shape[2]

    def copies(k):
        lanes = pl.ds(pl.multiple_of((start + k) * depth, depth), depth)
        return [
            pltpu.make_async_copy(w_hbm.at[lanes, :], w.at[k], w_sems.at[k]),
            pltpu.make_async_copy(x_hbm.at[:, lanes], x.at[k], x_sems.at[k]),
        ]

    return copies


def prefill_steps(start, copies, gain, x, w, acc, squares):
    chunks, rows, depth = x.shape

    def step(k, carry):
        for copy in copies(k):
            copy.wait()

        @pl.when(k + AHEAD < chunks)
        def _():
            for copy in copies(k + AHEAD):
                copy.start()

        scale = gain[pl.ds(pl.multiple_of((start + k) * depth, depth), depth)].reshape(1, depth)
        for r in range(rows // TALL):
            at = slice(r * TALL, (r + 1) * TALL)
            part = squares[at, :]
            scaled = []
            for n in range(depth // 128):
                lanes = slice(n * 128, (n + 1) * 128)
                tile = x[k, at, lanes]
                floats = tile.astype(F32)
                part = part + floats * floats
                scaled.append(tile * scale[:, lanes])
            squares[at, :] = part
            acc[at, :] += jnp.dot(
                jnp.concatenate(scaled, axis=1), w[k], preferred_element_type=F32
            )
        return carry

    lax.fori_loop(0, chunks, step, 0)


def prefill_scratch(rows, width, cols, chunks):
    depth = width // CHUNKS
    return [
        pltpu.VMEM((chunks, rows, depth), BF16),
        pltpu.VMEM((chunks, depth, cols), BF16),
        pltpu.VMEM((width,), BF16),
        pltpu.SemaphoreType.DMA((chunks,)),
        pltpu.SemaphoreType.DMA((chunks,)),
        pltpu.SemaphoreType.DMA((1,)),
    ]


def begin_kernel(
    kept_hbm, live_hbm, kv_hbm, x_hbm, gain_hbm, w_hbm,
    kv, bias, acc, squares,
    kept, live, small, blocks, x, w, gain, x_sems, w_sems, gain_sem,
):
    first = pltpu.make_async_copy(kept_hbm, kept, small.at[0])
    second = pltpu.make_async_copy(live_hbm, live, small.at[1])
    third = pltpu.make_async_copy(gain_hbm, gain, gain_sem.at[0])
    first.start()
    second.start()
    third.start()
    copies = prefill_copies(0, x_hbm, w_hbm, x, w, x_sems, w_sems)
    for k in range(min(AHEAD, x.shape[0])):
        for copy in copies(k):
            copy.start()
    acc[...] = jnp.zeros_like(acc)
    squares[...] = jnp.zeros_like(squares)
    first.wait()
    arriving = []
    for i in range(PRE):
        for t in range(KS):
            copy = pltpu.make_async_copy(kv_hbm.at[i, 0, kept[i, t]], kv.at[i, t], blocks.at[i, t])
            copy.start()
            arriving.append(copy)
    second.wait()
    token = lax.broadcasted_iota(jnp.int32, (1, KS * BLK), 1)
    for i in range(PRE):
        bias[i : i + 1, :] = jnp.where(token < live[i] * BLK, 0.0, -1e30)
    third.wait()
    prefill_steps(0, copies, gain, x, w, acc, squares)
    for copy in arriving:
        copy.wait()


def begin(kept, live, kv, x, gain, w):
    rows, width = x.shape
    cols = w.shape[1]
    return pl.pallas_call(
        begin_kernel,
        in_specs=[HBM] * 6,
        out_specs=[VMEM] * 4,
        out_shape=[
            pltpu.VMEM((PRE, KS, BLK, 2 * HD), BF16),
            pltpu.VMEM((PRE, KS * BLK), F32),
            pltpu.VMEM((rows, cols), F32),
            pltpu.VMEM((rows, 128), F32),
        ],
        scratch_shapes=[
            pltpu.SMEM(kept.shape, jnp.int32),
            pltpu.SMEM(live.shape, jnp.int32),
            pltpu.SemaphoreType.DMA((2,)),
            pltpu.SemaphoreType.DMA((PRE, KS)),
            *prefill_scratch(rows, width, cols, FIRST),
        ],
        compiler_params=pltpu.CompilerParams(vmem_limit_bytes=16 * 1024 * 1024),
        cost_estimate=pl.CostEstimate(
            flops=2 * rows * width * cols * FIRST // CHUNKS,
            bytes_accessed=(2 << 20) + 2 * (rows + cols) * width * FIRST // CHUNKS,
            transcendentals=0,
        ),
        name="begin",
    )(hbm(kept), hbm(live), hbm(kv), hbm(x), hbm(gain), hbm(w))


def finish_kernel(
    x_hbm, gain_hbm, w_hbm, weight_hbm, before, before_squares, after_ref,
    out_ref, held,
    acc, squares, held_sem, x, w, gain, x_sems, w_sems, gain_sem,
):
    third = pltpu.make_async_copy(gain_hbm, gain, gain_sem.at[0])
    third.start()
    copies = prefill_copies(FIRST, x_hbm, w_hbm, x, w, x_sems, w_sems)
    for k in range(min(AHEAD, x.shape[0])):
        for copy in copies(k):
            copy.start()
    weight = pltpu.make_async_copy(weight_hbm.at[pl.ds(0, held.shape[0]), :], held, held_sem.at[0])
    weight.start()
    acc[...] = before[...]
    squares[...] = before_squares[...]
    third.wait()
    prefill_steps(FIRST, copies, gain, x, w, acc, squares)
    mean = jnp.sum(squares[...], axis=1, keepdims=True) * (1.0 / x_hbm.shape[1])
    out_ref[...] = (acc[...] * lax.rsqrt(mean + EPS)).astype(BF16)
    weight.wait()


def finish(x, gain, w, weight, before, before_squares, after):
    rows, width = x.shape
    cols = w.shape[1]
    return pl.pallas_call(
        finish_kernel,
        in_specs=[HBM] * 4 + [VMEM] * 2 + [ANY],
        out_specs=[VMEM] * 2,
        out_shape=[
            jax.ShapeDtypeStruct((rows, cols), BF16),
            pltpu.VMEM((weight.shape[0] * HELD // GROUP, weight.shape[1]), BF16),
        ],
        scratch_shapes=[
            pltpu.VMEM((rows, cols), F32),
            pltpu.VMEM((rows, 128), F32),
            pltpu.SemaphoreType.DMA((1,)),
            *prefill_scratch(rows, width, cols, CHUNKS - FIRST),
        ],
        compiler_params=pltpu.CompilerParams(vmem_limit_bytes=20 * 1024 * 1024),
        cost_estimate=pl.CostEstimate(
            flops=2 * rows * width * cols * (CHUNKS - FIRST) // CHUNKS,
            bytes_accessed=2 * (rows + cols) * width * (CHUNKS - FIRST) // CHUNKS,
            transcendentals=0,
        ),
        name="finish",
    )(hbm(x), hbm(gain), hbm(w), hbm(weight), vmem(before), vmem(before_squares), after)


def attend_kernel(q0, q1, q2, q3, kv, bias, out_ref, turned):
    mine = lax.axis_index("pre")
    group = lax.axis_index("cache")
    lane = lax.broadcasted_iota(jnp.int32, (GROUP, HD), 1)
    for k, q_ref in zip(PEERS, (q0, q1, q2, q3)):
        for s in range(STEPS):
            floats = q_ref[s].astype(F32)
            for j in range(GROUP):
                at = (k * STEPS + s) * CACHE * GROUP + j
                turned[pl.ds(at, CACHE, stride=GROUP), :] = floats[:, j * HD : (j + 1) * HD]
    scores = []
    for k in range(PRE):
        blocks = []
        for s in range(STEPS):
            at = (k * STEPS + s) * CACHE * GROUP + group * GROUP
            blocks.append(turned[pl.ds(pl.multiple_of(at, GROUP), GROUP), :])
        blocks.append(jnp.zeros((GROUP, HD), F32))
        q = jnp.concatenate(blocks, axis=0).astype(BF16)
        keys = kv[mine ^ k, :, :, :HD].reshape(KS * BLK, HD)
        scores.append(
            lax.dot_general(q, keys, (((1,), (1,)), ((), ())), preferred_element_type=F32)
        )
    tops, totals, terms = [], [], []
    for k in range(PRE):
        biased = scores[k] * (1.0 / math.sqrt(HD)) + bias[pl.ds(mine ^ k, 1), :]
        top = jnp.max(biased, axis=1, keepdims=True).astype(BF16).astype(F32)
        term = jnp.exp(biased - top)
        tops.append(top)
        totals.append(jnp.sum(term, axis=1, keepdims=True))
        terms.append(term.astype(BF16))
    for k in range(PRE):
        values = kv[mine ^ k, :, :, HD:].reshape(KS * BLK, HD)
        weighted = jnp.dot(terms[k], values, preferred_element_type=F32) / totals[k]
        high = totals[k].astype(BF16).astype(F32)
        low = totals[k] - high
        figures = jnp.zeros((GROUP, HD), F32)
        for s in range(STEPS):
            rows = slice(s * GROUP, (s + 1) * GROUP)
            figures = jnp.where(lane == s, tops[k][rows], figures)
            figures = jnp.where(lane == s + 4, high[rows], figures)
            figures = jnp.where(lane == s + 8, low[rows], figures)
        message = jnp.concatenate([weighted[: STEPS * GROUP], figures], axis=0).astype(BF16)
        for c in range(CACHE):
            out_ref[(mine ^ k) * CACHE + c] = message


def attend(queries, kv, bias):
    return pl.pallas_call(
        attend_kernel,
        in_specs=[VMEM] * 6,
        out_specs=VMEM,
        out_shape=pltpu.VMEM((PRE * CACHE, SLOT * GROUP, HD), BF16),
        scratch_shapes=[pltpu.VMEM((PRE * STEPS * CACHE * GROUP, HD), F32)],
        compiler_params=pltpu.CompilerParams(vmem_limit_bytes=4 * 1024 * 1024),
        cost_estimate=pl.CostEstimate(
            flops=2 * PRE * 2 * 32 * 1024 * 128, bytes_accessed=1 << 21, transcendentals=1 << 17
        ),
        name="attend",
    )(*queries, vmem(kv), vmem(bias))


def project_kernel(parts_ref, held, w_hbm, keep_ref, give_ref, sheet, w, result, sems):
    wide = HD * HEAD
    copies = []
    for j in range(HELD, GROUP):
        copies.append(
            pltpu.make_async_copy(
                w_hbm.at[pl.ds(j * wide, wide), :], w.at[j - HELD], sems.at[j - HELD]
            )
        )
        copies[-1].start()
    sheet[...] = jnp.zeros_like(sheet)
    for c in range(CACHE):
        parts = [parts_ref[p * CACHE + c].astype(F32) for p in range(PRE)]
        figures = [part[STEPS * GROUP :] for part in parts]
        for s in range(STEPS):
            tops = [f[:, s : s + 1] for f in figures]
            totals = [f[:, s + 4 : s + 5] + f[:, s + 8 : s + 9] for f in figures]
            top = functools.reduce(jnp.maximum, tops)
            shares = [jnp.exp(t - top) * total for t, total in zip(tops, totals)]
            scale = 1.0 / functools.reduce(jnp.add, shares)
            joined = functools.reduce(
                jnp.add,
                [
                    (share * scale) * part[s * GROUP : (s + 1) * GROUP]
                    for share, part in zip(shares, parts)
                ],
            )
            sheet[pl.ds(s * CACHE + c, GROUP, stride=ROWS), :] = joined
    spread = (
        lax.broadcasted_iota(jnp.int32, (HD, wide), 1) // HEAD
        == lax.broadcasted_iota(jnp.int32, (HD, wide), 0)
    ).astype(BF16)
    repeated = jnp.dot(
        sheet[...].astype(BF16), spread, preferred_element_type=F32
    ).astype(BF16)
    block = lax.broadcasted_iota(jnp.int32, (ROWS, wide), 1) % HEAD
    total = jnp.zeros((HEAD * ROWS, keep_ref.shape[2]), F32)
    for j in range(GROUP):
        if j < HELD:
            weight = held[j * wide : (j + 1) * wide, :]
        else:
            copies[j - HELD].wait()
            weight = w[j - HELD]
        rows_j = repeated[j * ROWS : (j + 1) * ROWS, :]
        lhs = jnp.concatenate(
            [jnp.where(block == h, rows_j, jnp.zeros_like(rows_j)) for h in range(HEAD)], axis=0
        )
        total = total + jnp.dot(lhs, weight, preferred_element_type=F32)
    result[...] = total
    chip, core = lax.axis_index("head") // 2, lax.axis_index("head") % 2
    for t, (first, second) in enumerate(TURNS):
        mine = ((chip ^ (first + (second - first) * core)) * 2 + core) * ROWS
        other = ((chip ^ (second + (first - second) * core)) * 2 + 1 - core) * ROWS
        keep_ref[t] = result[pl.ds(pl.multiple_of(mine, ROWS), ROWS), :]
        give_ref[t] = result[pl.ds(pl.multiple_of(other, ROWS), ROWS), :].astype(BF16)


def project(parts, held, weight):
    cols = weight.shape[1]
    return pl.pallas_call(
        project_kernel,
        in_specs=[VMEM, VMEM, HBM],
        out_specs=[VMEM, VMEM],
        out_shape=[
            pltpu.VMEM((HEAD // 2, ROWS, cols), F32),
            pltpu.VMEM((HEAD // 2, ROWS, cols), BF16),
        ],
        scratch_shapes=[
            pltpu.VMEM((GROUP * ROWS, HD), F32),
            pltpu.VMEM((GROUP - HELD, HD * HEAD, cols), BF16),
            pltpu.VMEM((HEAD * ROWS, cols), F32),
            pltpu.SemaphoreType.DMA((GROUP - HELD,)),
        ],
        compiler_params=pltpu.CompilerParams(vmem_limit_bytes=8 * 1024 * 1024),
        cost_estimate=pl.CostEstimate(
            flops=2 * 128 * 8192 * 256, bytes_accessed=1 << 22, transcendentals=0
        ),
        name="project",
    )(parts, vmem(held), hbm(weight))


def total_kernel(a_ref, b_ref, c_ref, d_ref, out_ref):
    total = sum(ref[...].astype(F32) for ref in (b_ref, c_ref, d_ref)) + a_ref[...].astype(F32)
    for s in range(STEPS):
        out_ref[s] = total[s * CACHE : (s + 1) * CACHE].astype(BF16)


def total_of(terms):
    cols = terms[0].shape[1]
    return pl.pallas_call(
        total_kernel,
        in_specs=[VMEM] * 4,
        out_specs=VMEM,
        out_shape=jax.ShapeDtypeStruct((STEPS, CACHE, cols), BF16),
        compiler_params=pltpu.CompilerParams(vmem_limit_bytes=1024 * 1024),
        name="total",
    )(*terms)


def body(prompt_kv, kept, live_count, queries, out_weight, prefill_x, prefill_gain, kv_weight):
    queries = queries.reshape(STEPS, CACHE, GROUP * HD)
    around = {0: queries}
    for k in ORDER:
        around[k] = lax.ppermute(queries, "pre", [(i, i ^ k) for i in range(PRE)])
    taken = (prefill_x, prefill_gain, kv_weight.reshape(8192, 256))
    kv, bias, *begun = begin(kept.reshape(PRE, KS), live_count.reshape(PRE), prompt_kv, *taken)
    parts = attend([around[k] for k in PEERS], kv, bias)
    sent = lax.all_to_all(parts, ("pre", "cache"), split_axis=0, concat_axis=0, tiled=True)
    weight = out_weight.reshape(8192, 256)
    next_kv, held = finish(*taken, weight, *begun, parts)
    keep, give = project(sent, held, weight)
    got = lax.ppermute(give, "head", [(i, i ^ 1) for i in range(HEAD)])
    pairs = (keep + got.astype(F32)).astype(BF16)
    terms = [pairs[0]]
    for t in range(1, len(TURNS)):
        moves = [(i, i ^ (2 * TURNS[t][i % 2])) for i in range(HEAD)]
        terms.append(lax.ppermute(pairs[t], "head", moves))
    attended = total_of(terms)
    return (attended.reshape(STEPS, CACHE, 1, 256), next_kv.reshape(512, 1, 256))


def solution(mesh):
    in_specs = (
        P("cache", "head", "pre", None, None),
        P("cache", "head", "pre", None),
        P("cache", "head"),
        P(None, None, "pre", "head"),
        P("head", None, "cache", None),
        P(("pre", "cache"), None),
        P(),
        P(None, "head", None),
    )
    out_specs = (P(None, None, "pre", ("head", "cache")), P(("pre", "cache"), "head", None))
    return jax.shard_map(body, mesh=mesh, in_specs=in_specs, out_specs=out_specs, check_vma=False)
```
